32 devices in a mesh: section: 2 (over core), tensor: 4 (over y, x), dp: 4 (over z).
Axes of the slice: x: 2, y: 2, z: 4, core: 2. Of those that a mesh axis runs over, the one named last changes fastest.
Arguments:
- enc_resid: bfloat16 [256, 16, 2048], P(('section', 'tensor'), 'dp'), parts along dimension 1, may hold values from -6 to 6
- enc_branch: bfloat16 [256, 16, 2048], P(('section', 'tensor'), 'dp'), parts along dimension 1, may hold values from -4 to 4
- enc_gain: float32 [2048], replicated, may hold values from 0.1 to 1.9
- dec_in: bfloat16 [16, 128, 2048], P('dp', 'tensor'), parts along dimension 0, may hold values from -6 to 6
- q_weight: bfloat16 [2, 2048, 2048], P('section', None, 'tensor'), may hold values from -0.125 to 0.125
- kv_weight: bfloat16 [2, 2048, 2, 2048], P('section', None, None, 'tensor'), may hold values from -0.125 to 0.125
- out_weight: bfloat16 [2, 2048, 2048], P('section', 'tensor'), may hold values from -0.75 to 0.75
- temps: float32 [2, 8], P('section', 'tensor'), may hold values from 4 to 16
- enc_lengths: int32 [16], P('dp'), parts along dimension 0, may hold values from 1 to 256, 768 in all
Outputs:
- section_out: bfloat16 [2, 16, 128, 2048], P('section', 'dp', 'tensor'), parts along dimension 1
The draws below stay inside these ranges and needn't reach their ends.
There are 4 independent parts, one for each index of `dp`. The reference program is written for one: setup_inputs(seed, part) draws one part's arguments, and reference() takes and returns one part's arrays. A program takes and returns all parts, laid end to end along the dimension named above; an argument that names none is the same for every part. Nothing has to cross between parts.
Inputs may be any that keep to these rules, and one draw needn't show every extreme that they name: enc_lengths[m] is the number of unpadded encoder positions of sequence m; positions from it on are padding. Within each dp part (4 consecutive sequences), the lengths sum to 768 and one of them equals 256.
All inputs are finite; a program needn't handle non-finite values.
Results may differ from the reference program's by a relative error of at most 0.015.
Values may be sent and summed in bfloat16 or wider, within the bound.
A program may use at most 64 MiB of HBM per device.

```python
import math
import jax
import jax.numpy as jnp
import numpy as np
from jax import lax

D = 2048
H = 8
HD = 256
MICRO = 4
L_ENC = 256
L_DEC = 128
N_SECTION = 2
N_TENSOR = 4


def block_levels(key, shape, cuts, low, largest):
    factor_of = 1.0
    for dim, parts in cuts:
        draws = jax.random.uniform(jax.random.fold_in(jax.random.fold_in(key, 6), dim), (parts,), jnp.float32, low / len(cuts), largest / len(cuts))
        factor_of = factor_of * jnp.repeat(jnp.exp(draws), shape[dim] // parts).reshape((-1,) + (1,) * (len(shape) - 1 - dim))
    return factor_of


def split_up(number_of, total, reach, lean):
    loads = [(1 << 20) // math.isqrt(rank ** lean) + 1 for rank in range(2, number_of + 1)]
    surplus, given = total - reach - (number_of - 1), [1] * (number_of - 1)
    while surplus > 0:
        free = [i for i in range(number_of - 1) if given[i] < reach]
        pool, remaining = sum([loads[i] for i in free]), surplus
        for i in free:
            addition = min(reach - given[i], max(1, remaining * loads[i] // pool), surplus)
            given[i] = given[i] + addition
            surplus = surplus - addition
    return np.array([reach] + given)


def ragged_sizes(key, number_of, total, most, skew):
    if number_of == 2:
        one = jax.random.randint(key, (), max(1, total - most), min(most, total - 1) + 1)
        return jnp.stack([one, total - one])
    tallies = jnp.asarray(split_up(number_of, total, most, skew), jnp.int32)
    twos = (number_of - 1) // 2
    source_of, receiver = tallies[1:1 + 2 * twos:2], tallies[2:2 + 2 * twos:2]
    margin = jnp.minimum(source_of - 1, most - receiver)
    moved = jax.random.randint(jax.random.fold_in(key, 1), (twos,), 0, 1 << 20) % (margin + 1)
    tallies = tallies.at[1:1 + 2 * twos:2].set(source_of - moved).at[2:2 + 2 * twos:2].set(receiver + moved)
    return tallies[jax.random.permutation(jax.random.fold_in(key, 2), number_of)]


def noise(key, shape, width, bound, cuts=(), kind=jnp.bfloat16):
    values = width * jax.random.normal(key, shape, jnp.float32)
    if cuts:
        values = values * block_levels(key, shape, cuts, -0.22, 0.18)
    return jnp.clip(values, -bound, bound).astype(kind)


def setup_inputs(seed: int = 0, part: int = 0) -> dict:
    seeds = jax.random.split(jax.random.key(seed), 10)
    part_splits = jax.random.split(jax.random.fold_in(seeds[9], part), 10)
    enc_resid = noise(part_splits[0], (L_ENC, MICRO, D), 1.0, 6.0, ((0, 8),))
    enc_branch = noise(part_splits[1], (L_ENC, MICRO, D), 0.5, 4.0, ((0, 8),))
    enc_gain = jnp.clip(1.0 + 0.18 * jax.random.normal(seeds[2], (D,), jnp.float32), 0.1, 1.9)
    dec_in = noise(part_splits[3], (MICRO, L_DEC, D), 1.0, 6.0, ((1, 4),))
    q_weight = noise(seeds[4], (N_SECTION, D, H * HD), D ** -0.5, 0.125, ((0, 2), (2, 4)))
    kv_weight = noise(seeds[5], (N_SECTION, D, 2, H * HD), D ** -0.5, 0.125, ((0, 2), (3, 4)))
    out_weight = noise(seeds[6], (N_SECTION, H * HD, D), (H * HD // 32) ** -0.5, 0.75, ((0, 2), (1, 4)))
    temps = jnp.clip(jnp.exp(math.log(16.0) - 1.3862944 * jax.random.uniform(seeds[7], (N_SECTION, H), jnp.float32) ** block_levels(seeds[7], (N_SECTION, H), ((0, 2), (1, 4)), -0.2, 0.2)), 4.0, 16.0)
    enc_lengths = ragged_sizes(part_splits[8], MICRO, MICRO * L_ENC * 3 // 4, L_ENC, 1).astype(jnp.int32)
    return {"enc_resid": enc_resid, "enc_branch": enc_branch, "enc_gain": enc_gain, "dec_in": dec_in, "q_weight": q_weight, "kv_weight": kv_weight, "out_weight": out_weight, "temps": temps, "enc_lengths": enc_lengths}


EPS = 1e-06

def head_norm(values, size):
    shaped = values.reshape(values.shape[:-1] + (values.shape[-1] // size, size))
    factor = lax.rsqrt(lax.optimization_barrier(jnp.mean(shaped * shaped, axis=-1, keepdims=True)) + EPS)
    return (shaped * factor).astype(jnp.bfloat16)

def reference(enc_resid, enc_branch, enc_gain, dec_in, q_weight, kv_weight, out_weight, temps, enc_lengths):
    total = enc_resid.astype(jnp.float32) + enc_branch.astype(jnp.float32)
    factor = lax.rsqrt(lax.optimization_barrier(jnp.mean(total * total, axis=-1, keepdims=True)) + EPS)
    normed = (total * factor * enc_gain).astype(jnp.bfloat16)
    inner = H * HD
    group = inner // N_TENSOR
    positions = jnp.arange(L_ENC).astype(jnp.int32)
    valid = positions[None, :] < enc_lengths[:, None]
    state = dec_in
    layers = []
    for section in range(N_SECTION):
        joined = jnp.dot(normed.reshape(-1, D), kv_weight[section].reshape(D, 2 * inner), preferred_element_type=jnp.float32)
        joined = joined.astype(jnp.bfloat16).reshape(L_ENC, MICRO, 2 * inner)
        keys = head_norm(joined[..., :inner].astype(jnp.float32), HD)
        values = joined[..., inner:].reshape(L_ENC, MICRO, H, HD)
        query = jnp.dot(state.reshape(-1, D), q_weight[section], preferred_element_type=jnp.float32)
        query = head_norm(query.reshape(MICRO, L_DEC, inner), HD)
        scores = jnp.einsum('mqhd,kmhd->mhqk', query.astype(jnp.float32), keys.astype(jnp.float32))
        scores = scores * (temps[section][None, :, None, None] / HD)
        weights = jnp.where(valid[:, None, None, :], jnp.exp(scores), 0.0)
        probs = (weights / lax.optimization_barrier(jnp.sum(weights, axis=-1, keepdims=True))).astype(jnp.bfloat16)
        attended = jnp.einsum('mhqk,kmhd->mqhd', probs.astype(jnp.float32), values.astype(jnp.float32))
        attended = attended.astype(jnp.bfloat16).reshape(MICRO * L_DEC, inner)
        update = jnp.zeros((MICRO * L_DEC, D), jnp.float32)
        for index in range(N_TENSOR):
            partial_sum = jnp.dot(attended[:, index * group:(index + 1) * group], out_weight[section][index * group:(index + 1) * group], preferred_element_type=jnp.float32)
            update = update + partial_sum.astype(jnp.bfloat16).astype(jnp.float32)
        state = (state.astype(jnp.float32) + update.reshape(MICRO, L_DEC, D)).astype(jnp.bfloat16)
        layers.append(state)
    return jnp.stack(layers)
```

```python
import functools

import jax
import jax.numpy as jnp
from jax import lax
from jax.experimental import pallas as pl
from jax.experimental.pallas import tpu as pltpu
from jax.sharding import PartitionSpec as P

HD = 256
EPS = 1e-06
HALVES = 2
MESH = pl.DeviceIdType.MESH


def head_norm(values):
    factor = lax.rsqrt(jnp.mean(values * values, axis=-1, keepdims=True) + EPS)
    return (values * factor).astype(jnp.bfloat16)


def landed(ref, sem):
    pltpu.make_async_copy(ref, ref, sem).wait()


def kernel(
    sections, span, normed, dec, wq_hbm, wkv_hbm, wo_hbm, temps, lens, out,
    enc, wq, wkv, wo, kv, xg, part, pr, xs,
    own_sem, weight_sem, out_sem, enc_send, enc_recv, half_recv,
    x_own, x_first_send, x_next_send, x_recv, part_send, part_recv,
):
    section = lax.axis_index("section")
    tensor = lax.axis_index("tensor")
    micro, tensors, rows, width = xg.shape
    inner = wq.shape[1]
    heads = inner // HD
    per_half = micro // HALVES
    positions = tensors * sections * span
    half_width = width // 2
    peers = [tensor, tensor + 1 - 2 * lax.rem(tensor, 2), lax.rem(tensor + 2, 4), 3 - tensor]

    def remote(src, dst, send_sem, recv_sem, to_section, to_tensor):
        return pltpu.make_async_remote_copy(
            src_ref=src, dst_ref=dst, send_sem=send_sem, recv_sem=recv_sem,
            device_id={"section": to_section, "tensor": to_tensor}, device_id_type=MESH,
        )

    others = [lax.rem(section + k, sections) for k in range(1, sections)]

    for h in range(HALVES):
        pltpu.make_async_copy(normed.at[h], enc.at[h, 0, section], own_sem.at[h]).start()

    @pl.when(section == 0)
    def _():
        for m in range(micro):
            pltpu.make_async_copy(dec.at[m], xg.at[m, 0], x_own.at[m]).start()

    weights = [
        pltpu.make_async_copy(src, dst, weight_sem.at[i])
        for i, (src, dst) in enumerate(((wkv_hbm, wkv), (wq_hbm, wq), (wo_hbm, wo)))
    ]
    for copy in weights:
        copy.start()

    barrier = pltpu.get_barrier_semaphore()
    for to_section in [section] + others:
        for d in range(tensors):
            if d == 0 and to_section is section:
                continue
            pl.semaphore_signal(
                barrier, inc=1, device_id={"section": to_section, "tensor": peers[d]}, device_id_type=MESH
            )
    pl.semaphore_wait(barrier, sections * tensors - 1)

    started = []

    def send_block(h, d, place, copies):
        for k, other in enumerate(others):
            copies.append(
                remote(
                    enc.at[h, d, section], enc.at[h, d, section],
                    enc_send.at[h, place + k], enc_recv.at[h, d, section], other, tensor,
                )
            )

    def begin(copies):
        for copy in copies:
            copy.start()
        started.extend(copies)

    def send_own(h):
        landed(enc.at[h, 0, section], own_sem.at[h])
        copies = [
            remote(
                enc.at[h, 0, section], enc.at[h, d, section],
                enc_send.at[h, d - 1], enc_recv.at[h, d, section], section, peers[d],
            )
            for d in (1, 2)
        ]
        send_block(h, 0, 4, copies)
        begin(copies)

    def pass_on(h, d):
        landed(enc.at[h, d, section], enc_recv.at[h, d, section])
        columns = pl.ds((d - 1) * half_width, half_width)
        copies = [
            remote(
                enc.at[h, d, section, :, columns], enc.at[h, 3, section, :, columns],
                enc_send.at[h, 1 + d], half_recv.at[h, d - 1], section, peers[3 - d],
            )
        ]
        send_block(h, d, 4 + d * (sections - 1), copies)
        begin(copies)

    def pass_last(h):
        for i in range(2):
            landed(enc.at[h, 3, section, :, pl.ds(i * half_width, half_width)], half_recv.at[h, i])
        copies = []
        send_block(h, 3, 4 + 3 * (sections - 1), copies)
        begin(copies)

    def from_others(h):
        for d in range(tensors):
            for other in others:
                landed(enc.at[h, d, other], enc_recv.at[h, d, other])

    def first_copy(m, d):
        return remote(
            xg.at[m, 0], xg.at[m, d], x_first_send.at[m, d], x_recv.at[m, d], section, peers[d]
        )

    def send_first(which):
        @pl.when(section == 0)
        def _():
            for m in which:
                landed(xg.at[m, 0], x_own.at[m])
                for d in range(1, tensors):
                    first_copy(m, d).start()

    def project(h):
        block = enc.shape[3]

        @pl.loop(0, heads)
        def _(head):
            at_key = pl.multiple_of(head * HD, HD)
            at_value = pl.multiple_of(inner + head * HD, HD)
            joined = enc[h].reshape(tensors * sections * block, width)
            keys = jnp.dot(joined, wkv[:, pl.ds(at_key, HD)], preferred_element_type=jnp.float32)
            keys = head_norm(keys.astype(jnp.bfloat16).astype(jnp.float32)).astype(kv.dtype)
            values = jnp.dot(joined, wkv[:, pl.ds(at_value, HD)], preferred_element_type=jnp.float32)
            values = values.astype(jnp.bfloat16).astype(kv.dtype)
            for i in range(tensors * sections):
                for j in range(per_half):
                    place = (i * per_half + j) * span
                    target = (h * per_half + j, pl.ds(i * span, span))
                    kv[target + (pl.ds(at_key, HD),)] = keys[place:place + span]
                    kv[target + (pl.ds(at_value, HD),)] = values[place:place + span]

    row = lax.broadcasted_iota(jnp.int32, (1, positions), 1)
    distance = row // (sections * span)
    sender = jnp.where(
        distance == 0, peers[0], jnp.where(distance == 1, peers[1], jnp.where(distance == 2, peers[2], peers[3]))
    )
    place_of = ((row // span) % sections * tensors + sender) * span + row % span

    def part_copy(m, d):
        return remote(
            part.at[m, d], pr.at[m, d], part_send.at[m, d], part_recv.at[m, d], section, peers[d]
        )

    def next_copy(m, d):
        return remote(
            xs.at[m], xg.at[m, d], x_next_send.at[m, d], x_recv.at[m, d], section + 1, peers[d]
        )

    def attend(m):
        current = xg[m].reshape(tensors * rows, width)
        query = jnp.dot(current, wq[...], preferred_element_type=jnp.float32)
        valid = place_of < lens[m]
        attended = []
        for head in range(heads):
            at = head * HD
            query_n = head_norm(query[:, at:at + HD])
            keys_n = kv[m, :, at:at + HD].astype(jnp.bfloat16)
            values = kv[m, :, inner + at:inner + at + HD].astype(jnp.bfloat16)
            scores = lax.dot_general(
                query_n, keys_n, (((1,), (1,)), ((), ())), preferred_element_type=jnp.float32
            )
            unscaled = jnp.where(valid, jnp.exp(scores * (temps[0, head] / HD)), 0.0)
            probs = (unscaled / jnp.sum(unscaled, axis=-1, keepdims=True)).astype(jnp.bfloat16)
            attended.append(
                jnp.dot(probs, values, preferred_element_type=jnp.float32).astype(jnp.bfloat16)
            )
        attended = jnp.concatenate(attended, axis=1)
        partial = jnp.dot(attended, wo[...], preferred_element_type=jnp.float32).astype(jnp.bfloat16)
        part[m] = partial.reshape(tensors, rows, width)
        for d in range(1, tensors):
            part_copy(m, d).start()

    def finish(m):
        total = part[m, 0].astype(jnp.float32)
        for d in range(1, tensors):
            landed(pr.at[m, d], part_recv.at[m, d])
            total = total + pr[m, d].astype(jnp.float32)
        xs[m] = (xg[m, 0].astype(jnp.float32) + total).astype(jnp.bfloat16)

        @pl.when(section < sections - 1)
        def _():
            for d in range(tensors):
                next_copy(m, d).start()

        pltpu.make_async_copy(xs.at[m], out.at[m], out_sem.at[m]).start()

    send_own(0)
    send_first((0,))
    pass_on(0, 1)
    pass_on(0, 2)
    send_own(1)
    send_first(range(1, micro))
    pass_last(0)
    from_others(0)
    weights[0].wait()
    project(0)
    pass_on(1, 1)
    pass_on(1, 2)
    pass_last(1)
    from_others(1)
    project(1)
    weights[1].wait()
    weights[2].wait()

    @pl.loop(0, micro + 1)
    def _(step):
        @pl.when(step < micro)
        def _():
            @pl.when(section > 0)
            def _():
                landed(xg.at[step, 0], x_recv.at[step, 0])

            for d in range(1, tensors):
                landed(xg.at[step, d], x_recv.at[step, d])
            attend(step)

        @pl.when(step > 0)
        def _():
            finish(step - 1)

    for copy in started:
        copy.wait_send()

    @pl.loop(0, micro)
    def _(m):
        for d in range(1, tensors):
            part_copy(m, d).wait_send()
        pltpu.make_async_copy(xs.at[m], out.at[m], out_sem.at[m]).wait()

    @pl.when(section == 0)
    def _():
        @pl.loop(0, micro)
        def _(m):
            for d in range(1, tensors):
                first_copy(m, d).wait_send()

    @pl.when(section < sections - 1)
    def _():
        @pl.loop(0, micro)
        def _(m):
            for d in range(tensors):
                next_copy(m, d).wait_send()


def encoder_norm(enc_resid, enc_branch, enc_gain):
    total = enc_resid.astype(jnp.float32) + enc_branch.astype(jnp.float32)
    factor = lax.rsqrt(jnp.mean(total * total, axis=-1, keepdims=True) + EPS)
    return (total * factor * enc_gain).astype(jnp.bfloat16)


def local(
    enc_resid, enc_branch, enc_gain, dec_in, q_weight, kv_weight, out_weight, temps, enc_lengths
):
    sections = lax.axis_size("section")
    tensors = lax.axis_size("tensor")
    span, micro, width = enc_resid.shape
    rows = dec_in.shape[1]
    inner = q_weight.shape[2]
    block = micro // HALVES * span
    normed = encoder_norm(enc_resid, enc_branch, enc_gain)
    normed = normed.transpose(1, 0, 2).reshape(HALVES, block, width)
    kv_matrix = kv_weight[0].reshape(width, 2 * inner)
    positions = tensors * sections * span
    cache_type = jnp.bfloat16 if span % 16 == 0 else jnp.float32
    any_space = pl.BlockSpec(memory_space=pl.ANY)
    smem = pl.BlockSpec(memory_space=pltpu.SMEM)
    dma = pltpu.SemaphoreType.DMA
    bf16 = jnp.bfloat16
    tokens = micro * tensors * rows
    flops = 2 * micro * positions * width * 2 * inner + 4 * tokens * width * inner
    stored = pl.pallas_call(
        functools.partial(kernel, sections, span),
        out_shape=jax.ShapeDtypeStruct((micro, rows, width), bf16),
        in_specs=[any_space] * 5 + [smem] * 2,
        out_specs=any_space,
        scratch_shapes=[
            pltpu.VMEM((HALVES, tensors, sections, block, width), bf16),
            pltpu.VMEM((width, inner), bf16),
            pltpu.VMEM((width, 2 * inner), bf16),
            pltpu.VMEM((inner, width), bf16),
            pltpu.VMEM((micro, positions, 2 * inner), cache_type),
            pltpu.VMEM((micro, tensors, rows, width), bf16),
            pltpu.VMEM((micro, tensors, rows, width), bf16),
            pltpu.VMEM((micro, tensors, rows, width), bf16),
            pltpu.VMEM((micro, rows, width), bf16),
            dma((HALVES,)),
            dma((3,)),
            dma((micro,)),
            dma((HALVES, 4 + tensors * (sections - 1))),
            dma((HALVES, tensors, sections)),
            dma((HALVES, 2)),
            dma((micro,)),
            dma((micro, tensors)),
            dma((micro, tensors)),
            dma((micro, tensors)),
            dma((micro, tensors)),
            dma((micro, tensors)),
        ],
        compiler_params=pltpu.CompilerParams(
            collective_id=0, has_side_effects=True, vmem_limit_bytes=48 * 1024 * 1024
        ),
        cost_estimate=pl.CostEstimate(flops=flops, bytes_accessed=12 << 20, transcendentals=0),
    )(normed, dec_in, q_weight[0], kv_matrix, out_weight[0], temps, enc_lengths)
    return stored[None]


def solution(mesh):
    return jax.shard_map(
        local,
        mesh=mesh,
        in_specs=(
            P(("section", "tensor"), "dp", None),
            P(("section", "tensor"), "dp", None),
            P(),
            P("dp", "tensor", None),
            P("section", None, "tensor"),
            P("section", None, None, "tensor"),
            P("section", "tensor", None),
            P("section", "tensor"),
            P("dp"),
        ),
        out_specs=P("section", "dp", "tensor", None),
        check_vma=False,
    )
```

```python
import functools

import jax
import jax.numpy as jnp
from jax import lax
from jax.experimental import pallas as pl
from jax.experimental.pallas import tpu as pltpu
from jax.sharding import PartitionSpec as P

HD = 256
EPS = 1e-06
HALVES = 2
MESH = pl.DeviceIdType.MESH


def head_norm(values):
    factor = lax.rsqrt(jnp.mean(values * values, axis=-1, keepdims=True) + EPS)
    return (values * factor).astype(jnp.bfloat16)


def landed(ref, sem):
    pltpu.make_async_copy(ref, ref, sem).wait()


def kernel(
    sections, resid_hbm, branch_hbm, gain, dec, wq_hbm, wkv_hbm, wo_hbm, temps, lens, out,
    resid, branch, raw, enc, wq, wkv, wo, kv, xg, part, pr, xs,
    load_sem, weight_sem, out_sem, enc_send, enc_recv, half_recv,
    x_own, x_first_send, x_next_send, x_recv, part_send, part_recv,
):
    section = lax.axis_index("section")
    tensor = lax.axis_index("tensor")
    micro, tensors, rows, width = xg.shape
    span = resid.shape[0]
    inner = wq.shape[1]
    heads = inner // HD
    per_half = micro // HALVES
    positions = tensors * sections * span
    half_width = width // 2
    peers = [tensor, tensor + 1 - 2 * lax.rem(tensor, 2), lax.rem(tensor + 2, 4), 3 - tensor]

    def remote(src, dst, send_sem, recv_sem, to_section, to_tensor):
        return pltpu.make_async_remote_copy(
            src_ref=src, dst_ref=dst, send_sem=send_sem, recv_sem=recv_sem,
            device_id={"section": to_section, "tensor": to_tensor}, device_id_type=MESH,
        )

    others = [lax.rem(section + k, sections) for k in range(1, sections)]

    loads = [
        pltpu.make_async_copy(resid_hbm, resid, load_sem.at[0]),
        pltpu.make_async_copy(branch_hbm, branch, load_sem.at[1]),
    ]
    for copy in loads:
        copy.start()

    @pl.when(section == 0)
    def _():
        for m in range(micro):
            pltpu.make_async_copy(dec.at[m], xg.at[m, 0], x_own.at[m]).start()

    weights = [
        pltpu.make_async_copy(src, dst, weight_sem.at[i])
        for i, (src, dst) in enumerate(((wkv_hbm, raw), (wq_hbm, wq), (wo_hbm, wo)))
    ]
    for copy in weights:
        copy.start()

    barrier = pltpu.get_barrier_semaphore()
    for to_section in [section] + others:
        for d in range(tensors):
            if d == 0 and to_section is section:
                continue
            pl.semaphore_signal(
                barrier, inc=1, device_id={"section": to_section, "tensor": peers[d]}, device_id_type=MESH
            )

    for copy in loads:
        copy.wait()
    chunk = min(span, 16)
    for first in range(0, span, chunk):
        total = resid[first:first + chunk].astype(jnp.float32) + branch[first:first + chunk].astype(jnp.float32)
        factor = lax.rsqrt(jnp.mean(total * total, axis=-1, keepdims=True) + EPS)
        normed = total * factor * gain[...].reshape(1, 1, width)
        for m in range(micro):
            at = m % per_half * span + first
            enc[m // per_half, 0, section, at:at + chunk] = normed[:, m, :].astype(jnp.bfloat16)

    pl.semaphore_wait(barrier, sections * tensors - 1)

    started = []

    def send_block(h, d, place, copies):
        for k, other in enumerate(others):
            copies.append(
                remote(
                    enc.at[h, d, section], enc.at[h, d, section],
                    enc_send.at[h, place + k], enc_recv.at[h, d, section], other, tensor,
                )
            )

    def begin(copies):
        for copy in copies:
            copy.start()
        started.extend(copies)

    def send_own(h):
        copies = [
            remote(
                enc.at[h, 0, section], enc.at[h, d, section],
                enc_send.at[h, d - 1], enc_recv.at[h, d, section], section, peers[d],
            )
            for d in (1, 2)
        ]
        send_block(h, 0, 4, copies)
        begin(copies)

    def pass_on(h, d):
        landed(enc.at[h, d, section], enc_recv.at[h, d, section])
        columns = pl.ds((d - 1) * half_width, half_width)
        copies = [
            remote(
                enc.at[h, d, section, :, columns], enc.at[h, 3, section, :, columns],
                enc_send.at[h, 1 + d], half_recv.at[h, d - 1], section, peers[3 - d],
            )
        ]
        send_block(h, d, 4 + d * (sections - 1), copies)
        begin(copies)

    def pass_last(h):
        for i in range(2):
            landed(enc.at[h, 3, section, :, pl.ds(i * half_width, half_width)], half_recv.at[h, i])
        copies = []
        send_block(h, 3, 4 + 3 * (sections - 1), copies)
        begin(copies)

    def from_others(h):
        for d in range(tensors):
            for other in others:
                landed(enc.at[h, d, other], enc_recv.at[h, d, other])

    def first_copy(m, d):
        return remote(
            xg.at[m, 0], xg.at[m, d], x_first_send.at[m, d], x_recv.at[m, d], section, peers[d]
        )

    def send_first(which):
        @pl.when(section == 0)
        def _():
            for m in which:
                landed(xg.at[m, 0], x_own.at[m])
                for d in range(1, tensors):
                    first_copy(m, d).start()

    def project(h):
        block = enc.shape[3]

        @pl.loop(0, heads)
        def _(head):
            at_key = pl.multiple_of(head * HD, HD)
            at_value = pl.multiple_of(inner + head * HD, HD)
            joined = enc[h].reshape(tensors * sections * block, width)
            keys = jnp.dot(joined, wkv[:, pl.ds(at_key, HD)], preferred_element_type=jnp.float32)
            keys = head_norm(keys.astype(jnp.bfloat16).astype(jnp.float32)).astype(kv.dtype)
            values = jnp.dot(joined, wkv[:, pl.ds(at_value, HD)], preferred_element_type=jnp.float32)
            values = values.astype(jnp.bfloat16).astype(kv.dtype)
            for i in range(tensors * sections):
                for j in range(per_half):
                    place = (i * per_half + j) * span
                    target = (h * per_half + j, pl.ds(i * span, span))
                    kv[target + (pl.ds(at_key, HD),)] = keys[place:place + span]
                    kv[target + (pl.ds(at_value, HD),)] = values[place:place + span]

    row = lax.broadcasted_iota(jnp.int32, (1, positions), 1)
    distance = row // (sections * span)
    sender = jnp.where(
        distance == 0, peers[0], jnp.where(distance == 1, peers[1], jnp.where(distance == 2, peers[2], peers[3]))
    )
    place_of = ((row // span) % sections * tensors + sender) * span + row % span

    def part_copy(m, d):
        return remote(
            part.at[m, d], pr.at[m, d], part_send.at[m, d], part_recv.at[m, d], section, peers[d]
        )

    def next_copy(m, d):
        return remote(
            xs.at[m], xg.at[m, d], x_next_send.at[m, d], x_recv.at[m, d], section + 1, peers[d]
        )

    def attend(m):
        current = xg[m].reshape(tensors * rows, width)
        query = jnp.dot(current, wq[...], preferred_element_type=jnp.float32)
        valid = place_of < lens[m]
        attended = []
        for head in range(heads):
            at = head * HD
            query_n = head_norm(query[:, at:at + HD])
            keys_n = kv[m, :, at:at + HD].astype(jnp.bfloat16)
            values = kv[m, :, inner + at:inner + at + HD].astype(jnp.bfloat16)
            scores = lax.dot_general(
                query_n, keys_n, (((1,), (1,)), ((), ())), preferred_element_type=jnp.float32
            )
            unscaled = jnp.where(valid, jnp.exp(scores * (temps[0, head] / HD)), 0.0)
            probs = (unscaled / jnp.sum(unscaled, axis=-1, keepdims=True)).astype(jnp.bfloat16)
            attended.append(
                jnp.dot(probs, values, preferred_element_type=jnp.float32).astype(jnp.bfloat16)
            )
        attended = jnp.concatenate(attended, axis=1)
        partial = jnp.dot(attended, wo[...], preferred_element_type=jnp.float32).astype(jnp.bfloat16)
        part[m] = partial.reshape(tensors, rows, width)
        for d in range(1, tensors):
            part_copy(m, d).start()

    def finish(m):
        total = part[m, 0].astype(jnp.float32)
        for d in range(1, tensors):
            landed(pr.at[m, d], part_recv.at[m, d])
            total = total + pr[m, d].astype(jnp.float32)
        xs[m] = (xg[m, 0].astype(jnp.float32) + total).astype(jnp.bfloat16)

        @pl.when(section < sections - 1)
        def _():
            for d in range(tensors):
                next_copy(m, d).start()

        pltpu.make_async_copy(xs.at[m], out.at[m], out_sem.at[m]).start()

    def step(m):
        @pl.when(section > 0)
        def _():
            landed(xg.at[m, 0], x_recv.at[m, 0])

        for d in range(1, tensors):
            landed(xg.at[m, d], x_recv.at[m, d])
        attend(m)

    def split_weights():
        deep = 256

        @pl.loop(0, width // deep)
        def _(i):
            features = pl.ds(pl.multiple_of(i * deep, deep), deep)
            both = raw[features]
            wkv[features, :inner] = both[:, 0, :]
            wkv[features, inner:] = both[:, 1, :]

    def in_first(work, *which):
        @pl.when(section == 0)
        def _():
            for m in which:
                work(m)

    send_own(0)
    send_first((0,))
    weights[0].wait()
    split_weights()
    pass_on(0, 1)
    pass_on(0, 2)
    send_own(1)
    send_first((1,))
    pass_last(0)
    from_others(0)
    project(0)
    weights[1].wait()
    weights[2].wait()
    in_first(step, 0)
    pass_on(1, 1)
    pass_on(1, 2)
    send_first(range(2, micro))
    in_first(step, 1)
    pass_last(1)
    in_first(finish, 0)
    from_others(1)
    project(1)
    in_first(finish, 1)

    done = jnp.where(section == 0, 2, 0)

    @pl.loop(0, micro + 1)
    def _(now):
        @pl.when(jnp.logical_and(now >= done, now < micro))
        def _():
            step(now)

        @pl.when(now > done)
        def _():
            finish(now - 1)

    for copy in started:
        copy.wait_send()

    @pl.loop(0, micro)
    def _(m):
        for d in range(1, tensors):
            part_copy(m, d).wait_send()
        pltpu.make_async_copy(xs.at[m], out.at[m], out_sem.at[m]).wait()

    @pl.when(section == 0)
    def _():
        @pl.loop(0, micro)
        def _(m):
            for d in range(1, tensors):
                first_copy(m, d).wait_send()

    @pl.when(section < sections - 1)
    def _():
        @pl.loop(0, micro)
        def _(m):
            for d in range(tensors):
                next_copy(m, d).wait_send()


def local(
    enc_resid, enc_branch, enc_gain, dec_in, q_weight, kv_weight, out_weight, temps, enc_lengths
):
    sections = lax.axis_size("section")
    tensors = lax.axis_size("tensor")
    span, micro, width = enc_resid.shape
    rows = dec_in.shape[1]
    inner = q_weight.shape[2]
    block = micro // HALVES * span
    positions = tensors * sections * span
    cache_type = jnp.bfloat16 if span % 16 == 0 else jnp.float32
    any_space = pl.BlockSpec(memory_space=pl.ANY)
    vmem = pl.BlockSpec(memory_space=pltpu.VMEM)
    smem = pl.BlockSpec(memory_space=pltpu.SMEM)
    dma = pltpu.SemaphoreType.DMA
    bf16 = jnp.bfloat16
    tokens = micro * tensors * rows
    flops = 2 * micro * positions * width * 2 * inner + 4 * tokens * width * inner
    stored = pl.pallas_call(
        functools.partial(kernel, sections),
        out_shape=jax.ShapeDtypeStruct((micro, rows, width), bf16),
        in_specs=[any_space] * 2 + [vmem] + [any_space] * 4 + [smem] * 2,
        out_specs=any_space,
        scratch_shapes=[
            pltpu.VMEM((span, micro, width), bf16),
            pltpu.VMEM((span, micro, width), bf16),
            pltpu.VMEM((width, 2, inner), bf16),
            pltpu.VMEM((HALVES, tensors, sections, block, width), bf16),
            pltpu.VMEM((width, inner), bf16),
            pltpu.VMEM((width, 2 * inner), bf16),
            pltpu.VMEM((inner, width), bf16),
            pltpu.VMEM((micro, positions, 2 * inner), cache_type),
            pltpu.VMEM((micro, tensors, rows, width), bf16),
            pltpu.VMEM((micro, tensors, rows, width), bf16),
            pltpu.VMEM((micro, tensors, rows, width), bf16),
            pltpu.VMEM((micro, rows, width), bf16),
            dma((2,)),
            dma((3,)),
            dma((micro,)),
            dma((HALVES, 4 + tensors * (sections - 1))),
            dma((HALVES, tensors, sections)),
            dma((HALVES, 2)),
            dma((micro,)),
            dma((micro, tensors)),
            dma((micro, tensors)),
            dma((micro, tensors)),
            dma((micro, tensors)),
            dma((micro, tensors)),
        ],
        compiler_params=pltpu.CompilerParams(
            collective_id=0, has_side_effects=True, vmem_limit_bytes=48 * 1024 * 1024
        ),
        cost_estimate=pl.CostEstimate(flops=flops, bytes_accessed=12 << 20, transcendentals=0),
    )(
        enc_resid, enc_branch, enc_gain.reshape(1, width), dec_in,
        q_weight[0], kv_weight[0], out_weight[0], temps, enc_lengths,
    )
    return stored[None]


def solution(mesh):
    return jax.shard_map(
        local,
        mesh=mesh,
        in_specs=(
            P(("section", "tensor"), "dp", None),
            P(("section", "tensor"), "dp", None),
            P(),
            P("dp", "tensor", None),
            P("section", None, "tensor"),
            P("section", None, None, "tensor"),
            P("section", "tensor", None),
            P("section", "tensor"),
            P("dp"),
        ),
        out_specs=P("section", "dp", "tensor", None),
        check_vma=False,
    )
```

```python
import functools

import jax
import jax.numpy as jnp
from jax import lax
from jax.experimental import pallas as pl
from jax.experimental.pallas import tpu as pltpu
from jax.sharding import PartitionSpec as P

HD = 256
EPS = 1e-06
HALVES = 2
MESH = pl.DeviceIdType.MESH


def head_norm(values):
    factor = lax.rsqrt(jnp.mean(values * values, axis=-1, keepdims=True) + EPS)
    return (values * factor).astype(jnp.bfloat16)


def landed(ref, sem):
    pltpu.make_async_copy(ref, ref, sem).wait()


def kernel(
    sections, resid_hbm, branch_hbm, gain, dec, wq_hbm, wkv_hbm, wo_hbm, temps, lens, out,
    resid, branch, raw, enc, wq, wkv, wo, kv, xg, part, pr, xs,
    load_sem, weight_sem, out_sem, enc_send, enc_recv, half_recv,
    x_own, x_first_send, x_next_send, x_recv, x_pass_send, x_half_recv, part_send, part_recv,
):
    section = lax.axis_index("section")
    tensor = lax.axis_index("tensor")
    micro, tensors, rows, width = xg.shape
    span = resid.shape[0]
    inner = wq.shape[1]
    heads = inner // HD
    per_half = micro // HALVES
    positions = tensors * sections * span
    half_width = width // 2
    peers = [tensor, tensor + 1 - 2 * lax.rem(tensor, 2), lax.rem(tensor + 2, 4), 3 - tensor]

    def remote(src, dst, send_sem, recv_sem, to_section, to_tensor):
        return pltpu.make_async_remote_copy(
            src_ref=src, dst_ref=dst, send_sem=send_sem, recv_sem=recv_sem,
            device_id={"section": to_section, "tensor": to_tensor}, device_id_type=MESH,
        )

    others = [lax.rem(section + k, sections) for k in range(1, sections)]

    loads = [
        pltpu.make_async_copy(resid_hbm, resid, load_sem.at[0]),
        pltpu.make_async_copy(branch_hbm, branch, load_sem.at[1]),
    ]
    for copy in loads:
        copy.start()

    @pl.when(section == 0)
    def _():
        for m in range(micro):
            pltpu.make_async_copy(dec.at[m], xg.at[m, 0], x_own.at[m]).start()

    weights = [
        pltpu.make_async_copy(src, dst, weight_sem.at[i])
        for i, (src, dst) in enumerate(((wkv_hbm, raw), (wq_hbm, wq), (wo_hbm, wo)))
    ]
    for copy in weights:
        copy.start()

    barrier = pltpu.get_barrier_semaphore()
    for to_section in [section] + others:
        for d in range(tensors):
            if d == 0 and to_section is section:
                continue
            pl.semaphore_signal(
                barrier, inc=1, device_id={"section": to_section, "tensor": peers[d]}, device_id_type=MESH
            )

    for copy in loads:
        copy.wait()
    chunk = min(span, 16)
    for first in range(0, span, chunk):
        total = resid[first:first + chunk].astype(jnp.float32) + branch[first:first + chunk].astype(jnp.float32)
        factor = lax.rsqrt(jnp.mean(total * total, axis=-1, keepdims=True) + EPS)
        normed = total * factor * gain[...].reshape(1, 1, width)
        for m in range(micro):
            at = m % per_half * span + first
            enc[m // per_half, 0, section, at:at + chunk] = normed[:, m, :].astype(jnp.bfloat16)

    pl.semaphore_wait(barrier, sections * tensors - 1)

    started = []

    def send_block(h, d, place, copies):
        for k, other in enumerate(others):
            copies.append(
                remote(
                    enc.at[h, d, section], enc.at[h, d, section],
                    enc_send.at[h, place + k], enc_recv.at[h, d, section], other, tensor,
                )
            )

    def begin(copies):
        for copy in copies:
            copy.start()
        started.extend(copies)

    def send_own(h):
        copies = [
            remote(
                enc.at[h, 0, section], enc.at[h, d, section],
                enc_send.at[h, d - 1], enc_recv.at[h, d, section], section, peers[d],
            )
            for d in (1, 2)
        ]
        send_block(h, 0, 4, copies)
        begin(copies)

    def pass_on(h, d):
        landed(enc.at[h, d, section], enc_recv.at[h, d, section])
        columns = pl.ds((d - 1) * half_width, half_width)
        copies = [
            remote(
                enc.at[h, d, section, :, columns], enc.at[h, 3, section, :, columns],
                enc_send.at[h, 1 + d], half_recv.at[h, d - 1], section, peers[3 - d],
            )
        ]
        send_block(h, d, 4 + d * (sections - 1), copies)
        begin(copies)

    def pass_last(h):
        for i in range(2):
            landed(enc.at[h, 3, section, :, pl.ds(i * half_width, half_width)], half_recv.at[h, i])
        copies = []
        send_block(h, 3, 4 + 3 * (sections - 1), copies)
        begin(copies)

    def from_others(h):
        for d in range(tensors):
            for other in others:
                landed(enc.at[h, d, other], enc_recv.at[h, d, other])

    def first_copy(m, d):
        return remote(
            xg.at[m, 0], xg.at[m, d], x_first_send.at[m, d], x_recv.at[m, d], section, peers[d]
        )

    def send_first(which):
        @pl.when(section == 0)
        def _():
            for m in which:
                landed(xg.at[m, 0], x_own.at[m])
                for d in (1, 2):
                    first_copy(m, d).start()

    def project(h):
        block = enc.shape[3]

        @pl.loop(0, heads)
        def _(head):
            at_key = pl.multiple_of(head * HD, HD)
            at_value = pl.multiple_of(inner + head * HD, HD)
            joined = enc[h].reshape(tensors * sections * block, width)
            keys = jnp.dot(joined, wkv[:, pl.ds(at_key, HD)], preferred_element_type=jnp.float32)
            keys = head_norm(keys.astype(jnp.bfloat16).astype(jnp.float32)).astype(kv.dtype)
            values = jnp.dot(joined, wkv[:, pl.ds(at_value, HD)], preferred_element_type=jnp.float32)
            values = values.astype(jnp.bfloat16).astype(kv.dtype)
            for i in range(tensors * sections):
                for j in range(per_half):
                    place = (i * per_half + j) * span
                    target = (h * per_half + j, pl.ds(i * span, span))
                    kv[target + (pl.ds(at_key, HD),)] = keys[place:place + span]
                    kv[target + (pl.ds(at_value, HD),)] = values[place:place + span]

    row = lax.broadcasted_iota(jnp.int32, (1, positions), 1)
    distance = row // (sections * span)
    sender = jnp.where(
        distance == 0, peers[0], jnp.where(distance == 1, peers[1], jnp.where(distance == 2, peers[2], peers[3]))
    )
    place_of = ((row // span) % sections * tensors + sender) * span + row % span

    def part_copy(m, d):
        return remote(
            part.at[m, d], pr.at[m, d], part_send.at[m, d], part_recv.at[m, d], section, peers[d]
        )

    def next_copy(m, d):
        return remote(
            xs.at[m], xg.at[m, d], x_next_send.at[m, d], x_recv.at[m, d], section + 1, peers[d]
        )

    def pass_copy(m, d):
        columns = pl.ds((d - 1) * half_width, half_width)
        return remote(
            xg.at[m, d, :, columns], xg.at[m, 3, :, columns],
            x_pass_send.at[m, d - 1], x_half_recv.at[m, d - 1], section, peers[3 - d],
        )

    def relay(m):
        for d in (1, 2):
            landed(xg.at[m, d], x_recv.at[m, d])
            pass_copy(m, d).start()

    def attend(m):
        current = xg[m].reshape(tensors * rows, width)
        query = jnp.dot(current, wq[...], preferred_element_type=jnp.float32)
        valid = place_of < lens[m]
        attended = []
        for head in range(heads):
            at = head * HD
            query_n = head_norm(query[:, at:at + HD])
            keys_n = kv[m, :, at:at + HD].astype(jnp.bfloat16)
            values = kv[m, :, inner + at:inner + at + HD].astype(jnp.bfloat16)
            scores = lax.dot_general(
                query_n, keys_n, (((1,), (1,)), ((), ())), preferred_element_type=jnp.float32
            )
            unscaled = jnp.where(valid, jnp.exp(scores * (temps[0, head] / HD)), 0.0)
            probs = (unscaled / jnp.sum(unscaled, axis=-1, keepdims=True)).astype(jnp.bfloat16)
            attended.append(
                jnp.dot(probs, values, preferred_element_type=jnp.float32).astype(jnp.bfloat16)
            )
        attended = jnp.concatenate(attended, axis=1)
        partial = jnp.dot(attended, wo[...], preferred_element_type=jnp.float32).astype(jnp.bfloat16)
        part[m] = partial.reshape(tensors, rows, width)
        for d in range(1, tensors):
            part_copy(m, d).start()

    def finish(m):
        total = part[m, 0].astype(jnp.float32)
        for d in range(1, tensors):
            landed(pr.at[m, d], part_recv.at[m, d])
            total = total + pr[m, d].astype(jnp.float32)
        xs[m] = (xg[m, 0].astype(jnp.float32) + total).astype(jnp.bfloat16)

        @pl.when(section < sections - 1)
        def _():
            for d in range(tensors):
                next_copy(m, d).start()

        pltpu.make_async_copy(xs.at[m], out.at[m], out_sem.at[m]).start()

    def step(m):
        @pl.when(section > 0)
        def _():
            for d in range(tensors):
                landed(xg.at[m, d], x_recv.at[m, d])

        @pl.when(section == 0)
        def _():
            for i in range(2):
                landed(xg.at[m, 3, :, pl.ds(i * half_width, half_width)], x_half_recv.at[m, i])

        attend(m)

    def split_weights():
        deep = 256

        @pl.loop(0, width // deep)
        def _(i):
            features = pl.ds(pl.multiple_of(i * deep, deep), deep)
            both = raw[features]
            wkv[features, :inner] = both[:, 0, :]
            wkv[features, inner:] = both[:, 1, :]

    def in_first(work, *which):
        @pl.when(section == 0)
        def _():
            for m in which:
                work(m)

    send_own(0)
    send_first((0,))
    weights[0].wait()
    split_weights()
    pass_on(0, 1)
    pass_on(0, 2)
    in_first(relay, 0)
    send_own(1)
    send_first((1,))
    pass_last(0)
    from_others(0)
    project(0)
    weights[1].wait()
    weights[2].wait()
    in_first(step, 0)
    pass_on(1, 1)
    pass_on(1, 2)
    in_first(relay, 1)
    send_first(range(2, micro))
    in_first(step, 1)
    pass_last(1)
    in_first(finish, 0)
    from_others(1)
    in_first(relay, *range(2, micro))
    project(1)
    in_first(finish, 1)

    done = jnp.where(section == 0, 2, 0)

    @pl.loop(0, micro + 1)
    def _(now):
        @pl.when(jnp.logical_and(now >= done, now < micro))
        def _():
            step(now)

        @pl.when(now > done)
        def _():
            finish(now - 1)

    for copy in started:
        copy.wait_send()

    @pl.loop(0, micro)
    def _(m):
        for d in range(1, tensors):
            part_copy(m, d).wait_send()
        pltpu.make_async_copy(xs.at[m], out.at[m], out_sem.at[m]).wait()

    @pl.when(section == 0)
    def _():
        @pl.loop(0, micro)
        def _(m):
            for d in (1, 2):
                first_copy(m, d).wait_send()
                pass_copy(m, d).wait_send()

    @pl.when(section < sections - 1)
    def _():
        @pl.loop(0, micro)
        def _(m):
            for d in range(tensors):
                next_copy(m, d).wait_send()


def local(
    enc_resid, enc_branch, enc_gain, dec_in, q_weight, kv_weight, out_weight, temps, enc_lengths
):
    sections = lax.axis_size("section")
    tensors = lax.axis_size("tensor")
    span, micro, width = enc_resid.shape
    rows = dec_in.shape[1]
    inner = q_weight.shape[2]
    block = micro // HALVES * span
    positions = tensors * sections * span
    cache_type = jnp.bfloat16 if span % 16 == 0 else jnp.float32
    any_space = pl.BlockSpec(memory_space=pl.ANY)
    vmem = pl.BlockSpec(memory_space=pltpu.VMEM)
    smem = pl.BlockSpec(memory_space=pltpu.SMEM)
    dma = pltpu.SemaphoreType.DMA
    bf16 = jnp.bfloat16
    tokens = micro * tensors * rows
    flops = 2 * micro * positions * width * 2 * inner + 4 * tokens * width * inner
    stored = pl.pallas_call(
        functools.partial(kernel, sections),
        out_shape=jax.ShapeDtypeStruct((micro, rows, width), bf16),
        in_specs=[any_space] * 2 + [vmem] + [any_space] * 4 + [smem] * 2,
        out_specs=any_space,
        scratch_shapes=[
            pltpu.VMEM((span, micro, width), bf16),
            pltpu.VMEM((span, micro, width), bf16),
            pltpu.VMEM((width, 2, inner), bf16),
            pltpu.VMEM((HALVES, tensors, sections, block, width), bf16),
            pltpu.VMEM((width, inner), bf16),
            pltpu.VMEM((width, 2 * inner), bf16),
            pltpu.VMEM((inner, width), bf16),
            pltpu.VMEM((micro, positions, 2 * inner), cache_type),
            pltpu.VMEM((micro, tensors, rows, width), bf16),
            pltpu.VMEM((micro, tensors, rows, width), bf16),
            pltpu.VMEM((micro, tensors, rows, width), bf16),
            pltpu.VMEM((micro, rows, width), bf16),
            dma((2,)),
            dma((3,)),
            dma((micro,)),
            dma((HALVES, 4 + tensors * (sections - 1))),
            dma((HALVES, tensors, sections)),
            dma((HALVES, 2)),
            dma((micro,)),
            dma((micro, tensors)),
            dma((micro, tensors)),
            dma((micro, tensors)),
            dma((micro, 2)),
            dma((micro, 2)),
            dma((micro, tensors)),
            dma((micro, tensors)),
        ],
        compiler_params=pltpu.CompilerParams(
            collective_id=0, has_side_effects=True, vmem_limit_bytes=60 * 1024 * 1024
        ),
        cost_estimate=pl.CostEstimate(flops=flops, bytes_accessed=12 << 20, transcendentals=0),
    )(
        enc_resid, enc_branch, enc_gain.reshape(1, width), dec_in,
        q_weight[0], kv_weight[0], out_weight[0], temps, enc_lengths,
    )
    return stored[None]


def solution(mesh):
    return jax.shard_map(
        local,
        mesh=mesh,
        in_specs=(
            P(("section", "tensor"), "dp", None),
            P(("section", "tensor"), "dp", None),
            P(),
            P("dp", "tensor", None),
            P("section", None, "tensor"),
            P("section", None, None, "tensor"),
            P("section", "tensor", None),
            P("section", "tensor"),
            P("dp"),
        ),
        out_specs=P("section", "dp", "tensor", None),
        check_vma=False,
    )
```

```python
import functools

import jax
import jax.numpy as jnp
from jax import lax
from jax.experimental import pallas as pl
from jax.experimental.pallas import tpu as pltpu
from jax.sharding import PartitionSpec as P

HD = 256
EPS = 1e-06
HALVES = 2
MESH = pl.DeviceIdType.MESH


def head_norm(values):
    factor = lax.rsqrt(jnp.mean(values * values, axis=-1, keepdims=True) + EPS)
    return (values * factor).astype(jnp.bfloat16)


def landed(ref, sem):
    pltpu.make_async_copy(ref, ref, sem).wait()


def kernel(
    sections, resid_hbm, branch_hbm, gain, dec, wq_hbm, wkv_hbm, wo_hbm, temps, lens, out,
    resid, branch, raw, enc, wq, wkv, wo, kv, xg, part, pr, xs,
    load_sem, weight_sem, out_sem, enc_send, enc_recv, half_recv,
    x_own, x_first_send, x_next_send, x_recv, x_pass_send, x_half_recv, part_send, part_recv,
):
    section = lax.axis_index("section")
    tensor = lax.axis_index("tensor")
    micro, tensors, rows, width = xg.shape
    span = resid.shape[0]
    inner = wq.shape[1]
    heads = inner // HD
    per_half = micro // HALVES
    positions = tensors * sections * span
    half_width = width // 2
    peers = [tensor, tensor + 1 - 2 * lax.rem(tensor, 2), lax.rem(tensor + 2, 4), 3 - tensor]

    def remote(src, dst, send_sem, recv_sem, to_section, to_tensor):
        return pltpu.make_async_remote_copy(
            src_ref=src, dst_ref=dst, send_sem=send_sem, recv_sem=recv_sem,
            device_id={"section": to_section, "tensor": to_tensor}, device_id_type=MESH,
        )

    others = [lax.rem(section + k, sections) for k in range(1, sections)]

    loads = [
        pltpu.make_async_copy(resid_hbm, resid, load_sem.at[0]),
        pltpu.make_async_copy(branch_hbm, branch, load_sem.at[1]),
    ]
    for copy in loads:
        copy.start()

    @pl.when(section == 0)
    def _():
        for m in range(micro):
            pltpu.make_async_copy(dec.at[m], xg.at[m, 0], x_own.at[m]).start()

    weights = [
        pltpu.make_async_copy(src, dst, weight_sem.at[i])
        for i, (src, dst) in enumerate(((wkv_hbm, raw), (wq_hbm, wq), (wo_hbm, wo)))
    ]
    for copy in weights:
        copy.start()

    barrier = pltpu.get_barrier_semaphore()
    for to_section in [section] + others:
        for d in range(tensors):
            if d == 0 and to_section is section:
                continue
            pl.semaphore_signal(
                barrier, inc=1, device_id={"section": to_section, "tensor": peers[d]}, device_id_type=MESH
            )

    for copy in loads:
        copy.wait()
    chunk = min(span, 16)
    for first in range(0, span, chunk):
        total = resid[first:first + chunk].astype(jnp.float32) + branch[first:first + chunk].astype(jnp.float32)
        factor = lax.rsqrt(jnp.mean(total * total, axis=-1, keepdims=True) + EPS)
        normed = total * factor * gain[...].reshape(1, 1, width)
        for m in range(micro):
            at = m % per_half * span + first
            enc[m // per_half, 0, section, at:at + chunk] = normed[:, m, :].astype(jnp.bfloat16)

    pl.semaphore_wait(barrier, sections * tensors - 1)

    started = []

    def send_block(h, d, place, copies):
        for k, other in enumerate(others):
            copies.append(
                remote(
                    enc.at[h, d, section], enc.at[h, d, section],
                    enc_send.at[h, place + k], enc_recv.at[h, d, section], other, tensor,
                )
            )

    def begin(copies):
        for copy in copies:
            copy.start()
        started.extend(copies)

    def send_own(h):
        copies = [
            remote(
                enc.at[h, 0, section], enc.at[h, d, section],
                enc_send.at[h, d - 1], enc_recv.at[h, d, section], section, peers[d],
            )
            for d in (1, 2)
        ]
        send_block(h, 0, 4, copies)
        begin(copies)

    def pass_on(h, d):
        landed(enc.at[h, d, section], enc_recv.at[h, d, section])
        columns = pl.ds((d - 1) * half_width, half_width)
        copies = [
            remote(
                enc.at[h, d, section, :, columns], enc.at[h, 3, section, :, columns],
                enc_send.at[h, 1 + d], half_recv.at[h, d - 1], section, peers[3 - d],
            )
        ]
        send_block(h, d, 4 + d * (sections - 1), copies)
        begin(copies)

    def pass_last(h):
        for i in range(2):
            landed(enc.at[h, 3, section, :, pl.ds(i * half_width, half_width)], half_recv.at[h, i])
        copies = []
        send_block(h, 3, 4 + 3 * (sections - 1), copies)
        begin(copies)

    def from_others(h):
        for d in range(tensors):
            for other in others:
                landed(enc.at[h, d, other], enc_recv.at[h, d, other])

    def first_copy(m, d):
        return remote(
            xg.at[m, 0], xg.at[m, d], x_first_send.at[m, d], x_recv.at[m, d], section, peers[d]
        )

    def send_first(which):
        @pl.when(section == 0)
        def _():
            for m in which:
                landed(xg.at[m, 0], x_own.at[m])
                for d in (1, 2):
                    first_copy(m, d).start()

    def project(h):
        block = enc.shape[3]

        @pl.loop(0, heads)
        def _(head):
            at_key = pl.multiple_of(head * HD, HD)
            at_value = pl.multiple_of(inner + head * HD, HD)
            joined = enc[h].reshape(tensors * sections * block, width)
            keys = jnp.dot(joined, wkv[:, pl.ds(at_key, HD)], preferred_element_type=jnp.float32)
            keys = head_norm(keys.astype(jnp.bfloat16).astype(jnp.float32)).astype(kv.dtype)
            values = jnp.dot(joined, wkv[:, pl.ds(at_value, HD)], preferred_element_type=jnp.float32)
            values = values.astype(jnp.bfloat16).astype(kv.dtype)
            for i in range(tensors * sections):
                for j in range(per_half):
                    place = (i * per_half + j) * span
                    target = (h * per_half + j, pl.ds(i * span, span))
                    kv[target + (pl.ds(at_key, HD),)] = keys[place:place + span]
                    kv[target + (pl.ds(at_value, HD),)] = values[place:place + span]

    row = lax.broadcasted_iota(jnp.int32, (1, positions), 1)
    distance = row // (sections * span)
    sender = jnp.where(
        distance == 0, peers[0], jnp.where(distance == 1, peers[1], jnp.where(distance == 2, peers[2], peers[3]))
    )
    place_of = ((row // span) % sections * tensors + sender) * span + row % span

    def part_copy(m, d):
        return remote(
            part.at[m, d], pr.at[m, d], part_send.at[m, d], part_recv.at[m, d], section, peers[d]
        )

    def next_copy(m, d):
        return remote(
            xs.at[m], xg.at[m, d], x_next_send.at[m, d], x_recv.at[m, d], section + 1, peers[d]
        )

    def pass_copy(m, d):
        columns = pl.ds((d - 1) * half_width, half_width)
        return remote(
            xg.at[m, d, :, columns], xg.at[m, 3, :, columns],
            x_pass_send.at[m, d - 1], x_half_recv.at[m, d - 1], section, peers[3 - d],
        )

    def relay(m):
        for d in (1, 2):
            landed(xg.at[m, d], x_recv.at[m, d])
            pass_copy(m, d).start()

    def attend(m):
        current = xg[m].reshape(tensors * rows, width)
        query = jnp.dot(current, wq[...], preferred_element_type=jnp.float32)
        valid = place_of < lens[m]
        attended = []
        for head in range(heads):
            at = head * HD
            query_n = head_norm(query[:, at:at + HD])
            keys_n = kv[m, :, at:at + HD].astype(jnp.bfloat16)
            values = kv[m, :, inner + at:inner + at + HD].astype(jnp.bfloat16)
            scores = lax.dot_general(
                query_n, keys_n, (((1,), (1,)), ((), ())), preferred_element_type=jnp.float32
            )
            unscaled = jnp.where(valid, jnp.exp(scores * (temps[0, head] / HD)), 0.0)
            probs = (unscaled / jnp.sum(unscaled, axis=-1, keepdims=True)).astype(jnp.bfloat16)
            attended.append(
                jnp.dot(probs, values, preferred_element_type=jnp.float32).astype(jnp.bfloat16)
            )
        attended = jnp.concatenate(attended, axis=1)
        partial = jnp.dot(attended, wo[...], preferred_element_type=jnp.float32).astype(jnp.bfloat16)
        part[m] = partial.reshape(tensors, rows, width)
        for d in (3, 1, 2):
            part_copy(m, d).start()

    def finish(m):
        total = part[m, 0].astype(jnp.float32)
        for d in range(1, tensors):
            landed(pr.at[m, d], part_recv.at[m, d])
            total = total + pr[m, d].astype(jnp.float32)
        xs[m] = (xg[m, 0].astype(jnp.float32) + total).astype(jnp.bfloat16)

        @pl.when(section < sections - 1)
        def _():
            for d in (3, 1, 2, 0):
                next_copy(m, d).start()

        pltpu.make_async_copy(xs.at[m], out.at[m], out_sem.at[m]).start()

    def step(m):
        @pl.when(section > 0)
        def _():
            for d in range(tensors):
                landed(xg.at[m, d], x_recv.at[m, d])

        @pl.when(section == 0)
        def _():
            for i in range(2):
                landed(xg.at[m, 3, :, pl.ds(i * half_width, half_width)], x_half_recv.at[m, i])

        attend(m)

    def split_weights():
        deep = 256

        @pl.loop(0, width // deep)
        def _(i):
            features = pl.ds(pl.multiple_of(i * deep, deep), deep)
            both = raw[features]
            wkv[features, :inner] = both[:, 0, :]
            wkv[features, inner:] = both[:, 1, :]

    def in_first(work, *which):
        @pl.when(section == 0)
        def _():
            for m in which:
                work(m)

    send_own(0)
    send_first((0,))
    weights[0].wait()
    split_weights()
    pass_on(0, 1)
    pass_on(0, 2)
    in_first(relay, 0)
    send_own(1)
    send_first((1,))
    pass_last(0)
    from_others(0)
    project(0)
    weights[1].wait()
    weights[2].wait()
    in_first(step, 0)
    pass_on(1, 1)
    pass_on(1, 2)
    in_first(relay, 1)
    send_first(range(2, micro))
    in_first(step, 1)
    pass_last(1)
    in_first(finish, 0, 1)
    from_others(1)
    in_first(relay, *range(2, micro))
    project(1)

    done = jnp.where(section == 0, 2, 0)

    @pl.loop(0, micro + 1)
    def _(now):
        @pl.when(jnp.logical_and(now >= done, now < micro))
        def _():
            step(now)

        @pl.when(now > done)
        def _():
            finish(now - 1)

    for copy in started:
        copy.wait_send()

    @pl.loop(0, micro)
    def _(m):
        for d in range(1, tensors):
            part_copy(m, d).wait_send()
        pltpu.make_async_copy(xs.at[m], out.at[m], out_sem.at[m]).wait()

    @pl.when(section == 0)
    def _():
        @pl.loop(0, micro)
        def _(m):
            for d in (1, 2):
                first_copy(m, d).wait_send()
                pass_copy(m, d).wait_send()

    @pl.when(section < sections - 1)
    def _():
        @pl.loop(0, micro)
        def _(m):
            for d in range(tensors):
                next_copy(m, d).wait_send()


def local(
    enc_resid, enc_branch, enc_gain, dec_in, q_weight, kv_weight, out_weight, temps, enc_lengths
):
    sections = lax.axis_size("section")
    tensors = lax.axis_size("tensor")
    span, micro, width = enc_resid.shape
    rows = dec_in.shape[1]
    inner = q_weight.shape[2]
    block = micro // HALVES * span
    positions = tensors * sections * span
    cache_type = jnp.bfloat16 if span % 16 == 0 else jnp.float32
    any_space = pl.BlockSpec(memory_space=pl.ANY)
    vmem = pl.BlockSpec(memory_space=pltpu.VMEM)
    smem = pl.BlockSpec(memory_space=pltpu.SMEM)
    dma = pltpu.SemaphoreType.DMA
    bf16 = jnp.bfloat16
    tokens = micro * tensors * rows
    flops = 2 * micro * positions * width * 2 * inner + 4 * tokens * width * inner
    stored = pl.pallas_call(
        functools.partial(kernel, sections),
        out_shape=jax.ShapeDtypeStruct((micro, rows, width), bf16),
        in_specs=[any_space] * 2 + [vmem] + [any_space] * 4 + [smem] * 2,
        out_specs=any_space,
        scratch_shapes=[
            pltpu.VMEM((span, micro, width), bf16),
            pltpu.VMEM((span, micro, width), bf16),
            pltpu.VMEM((width, 2, inner), bf16),
            pltpu.VMEM((HALVES, tensors, sections, block, width), bf16),
            pltpu.VMEM((width, inner), bf16),
            pltpu.VMEM((width, 2 * inner), bf16),
            pltpu.VMEM((inner, width), bf16),
            pltpu.VMEM((micro, positions, 2 * inner), cache_type),
            pltpu.VMEM((micro, tensors, rows, width), bf16),
            pltpu.VMEM((micro, tensors, rows, width), bf16),
            pltpu.VMEM((micro, tensors, rows, width), bf16),
            pltpu.VMEM((micro, rows, width), bf16),
            dma((2,)),
            dma((3,)),
            dma((micro,)),
            dma((HALVES, 4 + tensors * (sections - 1))),
            dma((HALVES, tensors, sections)),
            dma((HALVES, 2)),
            dma((micro,)),
            dma((micro, tensors)),
            dma((micro, tensors)),
            dma((micro, tensors)),
            dma((micro, 2)),
            dma((micro, 2)),
            dma((micro, tensors)),
            dma((micro, tensors)),
        ],
        compiler_params=pltpu.CompilerParams(
            collective_id=0, has_side_effects=True, vmem_limit_bytes=60 * 1024 * 1024
        ),
        cost_estimate=pl.CostEstimate(flops=flops, bytes_accessed=12 << 20, transcendentals=0),
    )(
        enc_resid, enc_branch, enc_gain.reshape(1, width), dec_in,
        q_weight[0], kv_weight[0], out_weight[0], temps, enc_lengths,
    )
    return stored[None]


def solution(mesh):
    return jax.shard_map(
        local,
        mesh=mesh,
        in_specs=(
            P(("section", "tensor"), "dp", None),
            P(("section", "tensor"), "dp", None),
            P(),
            P("dp", "tensor", None),
            P("section", None, "tensor"),
            P("section", None, None, "tensor"),
            P("section", "tensor", None),
            P("section", "tensor"),
            P("dp"),
        ),
        out_specs=P("section", "dp", "tensor", None),
        check_vma=False,
    )
```
